32 devices in a mesh: member: 2 (over x), band: 16 (over z, y, core).
Axes of the slice: x: 2, y: 2, z: 4, core: 2. Of those that a mesh axis runs over, the one named last changes fastest.
Arguments:
- state: float32 [14, 6, 2048, 1024], P('member', None, 'band'), parts along dimension 0, may hold values from -6 to 6
- courant_lon: float32 [4096, 1024], P(('member', 'band')), parts along dimension 0, may hold values from 0.05 to 0.45
- courant_lat: float32 [4096, 1024], P(('member', 'band')), parts along dimension 0, may hold values from 0.05 to 0.45
- reference_field: float32 [12, 2048, 1024], P('member', 'band'), parts along dimension 0, may hold values from -6 to 6
- nudge_rate: float32 [512], replicated, may hold values from 0.05 to 1
Outputs:
- new_state: float32 [14, 6, 2048, 1024], P('member', None, 'band'), parts along dimension 0
The draws below stay inside these ranges and needn't reach their ends.
There are 2 independent parts, one for each index of `member`. The reference program is written for one: setup_inputs(seed, part) draws one part's arguments, and reference() takes and returns one part's arrays. A program takes and returns all parts, laid end to end along the dimension named above; an argument that names none is the same for every part. Nothing has to cross between parts.
All inputs are finite; a program needn't handle non-finite values.
Results may differ from the reference program's by a relative error of at most 0.0003.
Values sent between devices are 32-bit elements; how exact they have to be, the bound alone decides.
A program may use at most 256 MiB of HBM per device.

```python
import math
import jax
import jax.numpy as jnp
from jax import lax

NLON = 2048
NLAT = 1024
MW = 512
FIELDS = 7
LEV = 6
STEPS = 2


def levels(key, extent, shards, least, high):
    gain, own = 1.0, jax.random.fold_in(key, 6)
    for dim, parts in shards:
        draws = jnp.exp(jax.random.uniform(jax.random.fold_in(own, dim), (parts,), jnp.float32, least / len(shards), high / len(shards)))
        gain = gain * jnp.repeat(draws, extent[dim] // parts).reshape([-1 if axis == dim else 1 for axis in range(len(extent))])
    return gain


def noise(stream_key, extent, spread, reach, cuts=(), dtype=jnp.bfloat16):
    values = jax.random.normal(stream_key, extent, jnp.float32) * spread
    if len(cuts) > 0:
        values = levels(stream_key, extent, cuts, -0.22, 0.18) * values
    return jnp.clip(values, min=-reach, max=reach).astype(dtype)


def setup_inputs(seed: int = 0, part: int = 0) -> dict:
    arg_keys = jax.random.split(jax.random.key(seed), 6)
    own_keys = jax.random.split(jax.random.fold_in(arg_keys[5], part), 6)
    return {
        "state": noise(own_keys[0], (FIELDS, LEV, NLON, NLAT), 1.0, 6.0, ((2, 16),), jnp.float32),
        "courant_lon": jnp.clip(0.05 + 0.39999999 * jax.random.uniform(own_keys[1], (NLON, NLAT), jnp.float32) ** levels(own_keys[1], (NLON, NLAT), ((0, 16),), -0.2, 0.2), 0.05, 0.45),
        "courant_lat": jnp.clip(0.05 + 0.39999999 * jax.random.uniform(own_keys[2], (NLON, NLAT), jnp.float32) ** levels(own_keys[2], (NLON, NLAT), ((0, 16),), -0.2, 0.2), 0.05, 0.45),
        "reference_field": noise(own_keys[3], (LEV, NLON, NLAT), 1.0, 6.0, ((1, 16),), jnp.float32),
        "nudge_rate": jnp.clip(jnp.exp(jax.random.uniform(arg_keys[4], (MW,), jnp.float32, math.log(0.05), math.log(1.0))), 0.05, 1.0),
    }


highest = lax.Precision.HIGHEST

def latitude_terms(lat_total):
    centres = (jnp.arange(lat_total).astype(jnp.float32) + 0.5) * (math.pi / lat_total)
    return (jnp.cos(centres), jnp.log(jnp.sin(centres)), jnp.sin(centres) * (math.pi / lat_total))

def norm_table(wave_total):
    orders = jnp.arange(1, wave_total).astype(jnp.float32)
    terms = jnp.log((2.0 * orders + 1.0) / (2.0 * orders))
    return jnp.concatenate([jnp.zeros((1,), jnp.float32), jnp.cumsum(terms)])

def start_value(wave_ids, log_sin, norms):
    matches = wave_ids[:, None] == jnp.arange(norms.shape[0]).astype(jnp.int32)[None, :]
    log_norm = lax.optimization_barrier(jnp.sum(jnp.where(matches, norms[None, :], 0.0), axis=1))
    orders = wave_ids.astype(jnp.float32)
    return 0.5 * log_norm[:, None] + orders[:, None] * log_sin[None, :] - 0.5 * math.log(2.0)

def legendre_table(wave_rows, offset_rows, upper_rows, starts, cosines):

    def advance(carry, inputs):
        earlier, latest, deficit = carry
        wave_now, offset_now, upper_now = inputs
        orders = wave_now.astype(jnp.float32)[:, None]
        degree = (wave_now + offset_now).astype(jnp.float32)[:, None]
        factor_now = jnp.sqrt((4.0 * degree * degree - 1.0) / jnp.maximum(degree * degree - orders * orders, 1.0))
        below = degree - 1.0
        older_sq = jnp.where(offset_now[:, None] >= 2, (4.0 * below * below - 1.0) / jnp.maximum(below * below - orders * orders, 1.0), 1.0)
        factor_old = jnp.where(offset_now[:, None] >= 2, factor_now / jnp.sqrt(older_sq), 0.0)
        log_start = jnp.where(upper_now[:, None] == 1, starts[:, 1], starts[:, 0])
        clamped = jnp.maximum(log_start, -80.0)
        fresh = offset_now[:, None] == 0
        recurred = factor_now * cosines[None, :] * latest - factor_old * earlier
        largest = jnp.maximum(jnp.abs(recurred), jnp.abs(latest))
        absorb = jnp.maximum(deficit, -jnp.log(jnp.maximum(largest, 1.0)))
        rescale = jnp.exp(absorb)
        next_latest = jnp.where(fresh, jnp.exp(clamped), recurred * rescale)
        next_earlier = jnp.where(fresh, jnp.zeros_like(latest), latest * rescale)
        next_deficit = jnp.where(fresh, log_start - clamped, deficit - absorb)
        result_row = next_latest * jnp.exp(next_deficit)
        return ((next_earlier, next_latest, next_deficit), result_row)
    zero_row = jnp.zeros_like(starts[:, 0])
    final_carry, rows = lax.scan(advance, (zero_row, zero_row, zero_row), (wave_rows.T, offset_rows.T, upper_rows.T), unroll=16)
    return jnp.transpose(rows, (1, 0, 2))

def reference(state, courant_lon, courant_lat, reference_field, nudge_rate):
    advected = state
    for turn_index in range(STEPS):
        west_cells = jnp.roll(advected, 1, axis=2)
        south_cells = jnp.concatenate([jnp.zeros_like(advected[:, :, :, :1]), advected[:, :, :, :-1]], axis=3)
        advected = advected - courant_lon * (advected - west_cells) - courant_lat * (advected - south_cells)
    anomaly = reference_field - advected[0]
    spectrum = jnp.fft.rfft(anomaly, axis=1)[:, :MW] / NLON
    cosines, log_sin, quad_weights = latitude_terms(NLAT)
    norms = norm_table(MW)
    fourier = jnp.stack([jnp.real(spectrum), jnp.imag(spectrum)], axis=0)
    weighted = jnp.transpose(fourier, (2, 0, 1, 3)) * quad_weights
    group_size = 8
    grouped = weighted.reshape(MW // group_size, group_size, 2, LEV, NLAT)
    rate_padded = jnp.concatenate([nudge_rate, jnp.zeros((MW,), jnp.float32)])

    def one_group(inputs):
        wave_block, group_index = inputs
        wave_ids = group_index * group_size + jnp.arange(group_size).astype(jnp.int32)
        offsets = jnp.arange(MW).astype(jnp.int32)
        wave_rows = jnp.broadcast_to(wave_ids[:, None], (group_size, MW))
        offset_rows = jnp.broadcast_to(offsets[None, :], (group_size, MW))
        initial = start_value(wave_ids, log_sin, norms)
        legendre = legendre_table(wave_rows, offset_rows, jnp.zeros_like(wave_rows), jnp.stack([initial, initial], 1), cosines)
        degrees = wave_rows + offset_rows
        rate_rows = jnp.where(degrees < MW, jnp.take(rate_padded, degrees), 0.0)
        analysed = jnp.einsum('skj,sclj->skcl', legendre, wave_block, precision=highest)
        scaled = analysed * rate_rows[:, :, None, None]
        return jnp.einsum('skj,skcl->sclj', legendre, scaled, precision=highest)
    synthesised = lax.map(one_group, (grouped, jnp.arange(MW // group_size).astype(jnp.int32)))
    synthesised = synthesised.reshape(MW, 2, LEV, NLAT)
    pieces = jnp.transpose(synthesised, (1, 2, 0, 3))
    complex_spec = pieces[0] + 1j * pieces[1]
    padded = jnp.pad(complex_spec, ((0, 0), (0, NLON // 2 + 1 - MW), (0, 0)))
    increment = jnp.fft.irfft(padded, n=NLON, axis=1) * NLON
    nudged = advected[0] + increment
    return jnp.concatenate([nudged[None], advected[1:]], axis=0)
```

```python
import functools
import math

import jax
import jax.numpy as jnp
import numpy as np
from jax import lax
from jax.experimental import pallas as pl
from jax.experimental.pallas import tpu as pltpu
from jax.sharding import PartitionSpec as P

STEPS = 2
SHIFT = 44.0
GROUP = 8
ROWS = 16
VMEM = 56 * 1024 * 1024


def passed_along(value, axis, by):
    peers = lax.axis_size(axis)
    return lax.ppermute(value, axis, [(i, (i + by) % peers) for i in range(peers)])


def prepare(lon_ref, lat_ref, keep, south, lanes):
    first = lanes == 0
    for r in range(0, keep.shape[0], 8):
        cl = lon_ref[r : r + 8, :]
        ct = lat_ref[r : r + 8, :]
        keep[r : r + 8, :] = 1.0 - cl - ct
        south[r : r + 8, :] = jnp.where(first, 0.0, ct)


def two_steps(read, halo, edge_ref, lon_ref, keep, south, rows, lanes, emit):
    lat = keep.shape[1]
    top = rows == 0
    far = jnp.broadcast_to(halo[0:1, :], (8, lat))
    near = jnp.broadcast_to(halo[1:2, :], (8, lat))
    edge_lon = jnp.broadcast_to(edge_ref[0:1, :], (8, lat))
    edge_lat = jnp.broadcast_to(edge_ref[1:2, :], (8, lat))
    edge_keep = 1.0 - edge_lon - edge_lat
    edge_south = jnp.where(lanes == 0, 0.0, edge_lat)
    west0 = near
    west1 = edge_keep * near + edge_lon * far + edge_south * pltpu.roll(near, 1, 1)
    for r in range(0, keep.shape[0], 8):
        cells = read(r)
        ck = keep[r : r + 8, :]
        cs = south[r : r + 8, :]
        cl = lon_ref[r : r + 8, :]
        turned = pltpu.roll(cells, 1, 0)
        once = ck * cells + cl * jnp.where(top, west0, turned) + cs * pltpu.roll(cells, 1, 1)
        west0 = turned
        turned = pltpu.roll(once, 1, 0)
        twice = ck * once + cl * jnp.where(top, west1, turned) + cs * pltpu.roll(once, 1, 1)
        west1 = turned
        emit(r, twice)


def iotas(lat):
    return (
        lax.broadcasted_iota(jnp.int32, (8, lat), 0),
        lax.broadcasted_iota(jnp.int32, (8, lat), 1),
    )


def first_kernel(s_ref, h_ref, e_ref, lon_ref, lat_ref, f_ref, a_ref, t_ref, keep, south, diff):
    rows, lanes = iotas(keep.shape[1])

    @pl.when(pl.program_id(0) == 0)
    def _():
        prepare(lon_ref, lat_ref, keep, south, lanes)

    def emit(r, chunk):
        a_ref[0, r : r + 8, :] = chunk
        diff[r : r + 8, :] = f_ref[0, r : r + 8, :] - chunk

    two_steps(
        lambda r: s_ref[0, 0, r : r + 8, :], h_ref[0], e_ref, lon_ref, keep, south, rows, lanes, emit
    )
    t_ref[:, 0] = diff[...].T.reshape(t_ref.shape[0], t_ref.shape[2], t_ref.shape[3])


def rest_kernel(s_ref, h_ref, e_ref, lon_ref, lat_ref, o_ref, keep, south):
    rows, lanes = iotas(keep.shape[1])

    @pl.when((pl.program_id(0) == 0) & (pl.program_id(1) == 0))
    def _():
        prepare(lon_ref, lat_ref, keep, south, lanes)

    def one_level(i, carry):
        def emit(r, chunk):
            o_ref[0, i, r : r + 8, :] = chunk

        two_steps(
            lambda r: s_ref[0, i, r : r + 8, :],
            h_ref[0, i],
            e_ref,
            lon_ref,
            keep,
            south,
            rows,
            lanes,
            emit,
        )
        return carry

    lax.fori_loop(0, s_ref.shape[1], one_level, 0)


def last_kernel(a_ref, t_ref, b_ref, o_ref):
    lon, lat = a_ref.shape[1], a_ref.shape[2]
    o_ref[0, 0] = a_ref[0] + t_ref[:, 0].reshape(lat, lon).T


def table_kernel(start_ref, wave_ref, mu_ref, out_ref):
    half = mu_ref.shape[1]
    tiles = half // 128
    start = start_ref[...]
    mu = jnp.broadcast_to(mu_ref[...], (GROUP, half))
    wave = wave_ref[...]
    count = jnp.maximum(jnp.floor(start * (-1.0 / SHIFT)), 0.0)
    latest = jnp.exp(start + count * SHIFT)
    earlier = jnp.zeros_like(latest)
    before = jnp.ones_like(wave)

    def block(i, carry):
        latest, earlier, count, before = carry
        scale = jnp.exp(count * -SHIFT)
        for k in range(16):
            at = pl.multiple_of((i * 8 + k // 2) * GROUP, GROUP)
            row = latest * scale
            for c in range(tiles):
                out_ref[k % 2, c, pl.ds(at, GROUP), :] = row[:, c * 128 : (c + 1) * 128]
            offset = (i * 16 + (k + 1)).astype(jnp.float32)
            degree = wave + offset
            square = (4.0 * degree * degree - 1.0) / (offset * (degree + wave))
            factor = jnp.sqrt(square)
            older = factor / before
            before = factor
            wide = jnp.concatenate([factor] * tiles, axis=1)
            wide_old = jnp.concatenate([older] * tiles, axis=1)
            latest, earlier = wide * (mu * latest) - wide_old * earlier, latest
        grown = (jnp.maximum(jnp.abs(latest), jnp.abs(earlier)) > 1.0) & (count > 0.5)
        down = jnp.where(grown, math.exp(-SHIFT), 1.0)
        return latest * down, earlier * down, jnp.where(grown, count - 1.0, count), before

    lax.fori_loop(0, out_ref.shape[2] // (8 * GROUP), block, (latest, earlier, count, before))


def parts(x):
    high = x.astype(jnp.bfloat16)
    return high, (x - high.astype(jnp.float32)).astype(jnp.bfloat16)


def dot(a, b, dims):
    return lax.dot_general(a, b, (dims, ((), ())), preferred_element_type=jnp.float32)


def mirrored(x, flip):
    high, low = parts(x)
    both = ((1,), (0,))
    return dot(high, flip, both) + dot(low, flip, both)


def transform_kernel(first, stride, f_ref, p_ref, r_ref, q_ref, j_ref, o_ref, even, odd):
    half = q_ref.shape[1]
    flip = j_ref[...]
    quad = q_ref[...]
    north = f_ref[:, :half]
    turned = mirrored(f_ref[:, half:], flip)
    even[...] = (north + turned) * quad
    odd[...] = (north - turned) * quad
    length = p_ref.shape[2] // GROUP
    for m in range(GROUP):
        sums = []
        for p, side in ((0, even), (1, odd)):
            f_high, f_low = parts(side[m * ROWS : (m + 1) * ROWS, :])
            table = [
                p_ref[p, c, pl.ds(m, length, stride=GROUP), :] for c in range(p_ref.shape[1])
            ]
            p_high, p_low = parts(jnp.concatenate(table, axis=1))
            across, along = ((1,), (1,)), ((1,), (0,))
            pair = dot(jnp.concatenate([f_high, f_low], axis=0), p_high, across)
            coeffs = pair[:ROWS] + pair[ROWS:] + dot(f_high, p_low, across)
            at = (first + m) * stride
            c_high, c_low = parts(coeffs * r_ref[p : p + 1, at : at + length])
            pair = dot(jnp.concatenate([c_high, c_low], axis=0), p_high, along)
            sums.append(pair[:ROWS] + pair[ROWS:] + dot(c_high, p_low, along))
        o_ref[m * ROWS : (m + 1) * ROWS, :half] = sums[0] + sums[1]
        even[m * ROWS : (m + 1) * ROWS, :] = sums[0] - sums[1]
    o_ref[:, half:] = mirrored(even[...], flip)


def cost(flops, moved):
    return pl.CostEstimate(flops=int(flops), bytes_accessed=int(moved), transcendentals=0)


def body(state, courant_lon, courant_lat, reference_field, nudge_rate):
    fields, levels, lon, lat = state.shape
    bands = lax.axis_size("band")
    place = lax.axis_index("band")
    lon_total = lon * bands
    lat_local = lat // bands
    waves = nudge_rate.shape[0]
    wave_local = waves // bands
    groups = wave_local // GROUP
    half = lat // 2
    params = functools.partial(pltpu.CompilerParams, vmem_limit_bytes=VMEM)
    f32 = jnp.float32

    edges = passed_along(jnp.concatenate([courant_lon[-1:], courant_lat[-1:]], axis=0), "band", 1)
    halo0 = passed_along(state[0, :, -2:], "band", 1)
    halo1 = passed_along(state[1:, :, -2:], "band", 1)

    whole2 = lambda *_: (0, 0)
    courant_specs = [
        pl.BlockSpec((2, lat), whole2),
        pl.BlockSpec((lon, lat), whole2),
        pl.BlockSpec((lon, lat), whole2),
    ]
    coef_scratch = [pltpu.VMEM((lon, lat), f32), pltpu.VMEM((lon, lat), f32)]
    cells = levels * lon * lat
    advected0, turned = pl.pallas_call(
        first_kernel,
        grid=(levels,),
        in_specs=[
            pl.BlockSpec((1, 1, lon, lat), lambda v: (0, v, 0, 0)),
            pl.BlockSpec((1, 2, lat), lambda v: (v, 0, 0)),
            *courant_specs,
            pl.BlockSpec((1, lon, lat), lambda v: (v, 0, 0)),
        ],
        out_specs=[
            pl.BlockSpec((1, lon, lat), lambda v: (v, 0, 0)),
            pl.BlockSpec((bands, 1, lat_local, lon), lambda v: (0, v, 0, 0)),
        ],
        out_shape=[
            jax.ShapeDtypeStruct((levels, lon, lat), f32),
            jax.ShapeDtypeStruct((bands, levels, lat_local, lon), f32),
        ],
        scratch_shapes=[*coef_scratch, pltpu.VMEM((lon, lat), f32)],
        compiler_params=params(),
        cost_estimate=cost(cells * 14, cells * 16),
        name="advect_first",
    )(state, halo0, edges, courant_lon, courant_lat, reference_field)

    spread = lax.all_to_all(turned, "band", 0, 0, tiled=True)

    per = 3 if levels % 3 == 0 else 1
    partial = pl.pallas_call(
        rest_kernel,
        grid=(fields - 1, levels // per),
        in_specs=[
            pl.BlockSpec((1, per, lon, lat), lambda f, v: (f + 1, v, 0, 0)),
            pl.BlockSpec((1, per, 2, lat), lambda f, v: (f, v, 0, 0)),
            *courant_specs,
        ],
        out_specs=pl.BlockSpec((1, per, lon, lat), lambda f, v: (f + 1, v, 0, 0)),
        out_shape=jax.ShapeDtypeStruct(state.shape, f32),
        scratch_shapes=coef_scratch,
        compiler_params=params(),
        cost_estimate=cost((fields - 1) * cells * 14, (fields - 1) * cells * 8),
        name="advect_rest",
    )(state, halo1, edges, courant_lon, courant_lat)

    order = (np.arange(bands)[:, None] + bands * np.arange(wave_local)[None, :]).reshape(-1)
    angle = (order[:, None] * np.arange(lon_total)[None, :] % lon_total) * (2.0 * np.pi / lon_total)
    waves_np = np.stack([np.cos(angle), -np.sin(angle)], axis=1).reshape(2 * waves, lon_total)
    forward = jnp.asarray((waves_np / lon_total).astype(np.float32))
    doubling = np.repeat(np.where(order == 0, 1.0, 2.0), 2)[:, None]
    inverse = jnp.asarray((waves_np * doubling).astype(np.float32))
    theta = np.pi * (np.arange(half) + 0.5) / lat
    mu = jnp.asarray(np.cos(theta)[None].astype(np.float32))
    quad = jnp.asarray((np.sin(theta) * np.pi / lat)[None].astype(np.float32))
    log_sin = jnp.asarray(np.log(np.sin(theta)).astype(np.float32))
    k = np.arange(1, waves)
    norms = np.concatenate([[0.0], np.cumsum(np.log((2.0 * k + 1.0) / (2.0 * k)))])
    norms = norms.reshape(wave_local, bands).T.astype(np.float32)
    own_norm = lax.dynamic_slice_in_dim(jnp.asarray(norms), place, 1, 0)[0]
    own_wave = (place + bands * jnp.arange(wave_local)).astype(f32)
    starts = 0.5 * own_norm[:, None] + own_wave[:, None] * log_sin[None] - 0.5 * math.log(2.0)
    wide_wave = jnp.broadcast_to(own_wave[:, None], (wave_local, 128))
    flip = jnp.asarray(np.eye(half)[::-1].astype(np.float32)).astype(jnp.bfloat16)
    own_rate = lax.dynamic_slice_in_dim(
        jnp.concatenate([nudge_rate, jnp.zeros((waves + bands,), f32)]), place, 2 * waves, 0
    )

    own_rate = own_rate.reshape(waves, 2).T

    tables = []
    for g in range(groups):
        depth = waves - bands * GROUP * g
        depth = -(-depth // 16) * 16
        at = slice(g * GROUP, (g + 1) * GROUP)
        tables.append(
            pl.pallas_call(
                table_kernel,
                out_shape=jax.ShapeDtypeStruct((2, half // 128, depth // 2 * GROUP, 128), f32),
                compiler_params=params(),
                cost_estimate=cost(depth * GROUP * half * 8, depth * GROUP * half * 4),
                name="legendre_table",
            )(starts[at], wide_wave[at], mu)
        )

    fourier = lax.dot_general(
        forward.reshape(2 * waves, bands, lon),
        spread,
        (((1, 2), (0, 3)), ((), ())),
        precision=lax.Precision.HIGH,
    )
    fourier = fourier.reshape(bands, 2 * wave_local, levels * lat_local)
    owned = lax.all_to_all(fourier, "band", 0, 0, tiled=True)
    owned = owned.reshape(bands, wave_local, 2, levels, lat_local).transpose(1, 2, 3, 0, 4)
    owned = owned.reshape(wave_local, 2 * levels, lat)
    owned = jnp.pad(owned, ((0, 0), (0, ROWS - 2 * levels), (0, 0)))

    synth = []
    for g in range(groups):
        length = tables[g].shape[2] // GROUP
        block = owned[g * GROUP : (g + 1) * GROUP].reshape(GROUP * ROWS, lat)
        synth.append(
            pl.pallas_call(
                functools.partial(transform_kernel, g * GROUP, bands // 2),
                out_shape=jax.ShapeDtypeStruct((GROUP * ROWS, lat), f32),
                scratch_shapes=[pltpu.VMEM((GROUP * ROWS, half), f32)] * 2,
                compiler_params=params(),
                cost_estimate=cost(length * GROUP * half * 400, length * GROUP * half * 8),
                name="legendre_transform",
            )(block, tables[g], own_rate, quad, flip)
        )
    waves_out = jnp.concatenate(synth, axis=0).reshape(wave_local, ROWS, lat)[:, : 2 * levels]
    waves_out = waves_out.reshape(wave_local, 2, levels, bands, lat_local).transpose(3, 0, 1, 2, 4)
    waves_out = waves_out.reshape(bands, 2 * wave_local, levels * lat_local)
    gathered = lax.all_to_all(waves_out, "band", 0, 0, tiled=True)
    gathered = gathered.reshape(2 * waves, levels * lat_local)
    increment = lax.dot_general(
        gathered, inverse, (((0,), (0,)), ((), ())), precision=lax.Precision.HIGH
    )
    increment = increment.reshape(levels * lat_local, bands, lon).transpose(1, 0, 2)
    increment = increment.reshape(bands, levels, lat_local, lon)
    increment = lax.all_to_all(increment, "band", 0, 0, tiled=True)

    return pl.pallas_call(
        last_kernel,
        grid=(levels,),
        in_specs=[
            pl.BlockSpec((1, lon, lat), lambda v: (v, 0, 0)),
            pl.BlockSpec((bands, 1, lat_local, lon), lambda v: (0, v, 0, 0)),
            pl.BlockSpec(memory_space=pl.ANY),
        ],
        out_specs=pl.BlockSpec((1, 1, lon, lat), lambda v: (0, v, 0, 0)),
        out_shape=jax.ShapeDtypeStruct(state.shape, f32),
        input_output_aliases={2: 0},
        compiler_params=params(),
        cost_estimate=cost(cells, cells * 12),
        name="add_increment",
    )(advected0, increment, partial)


def solution(mesh):
    placed = (
        P("member", None, "band", None),
        P(("member", "band"), None),
        P(("member", "band"), None),
        P("member", "band", None),
        P(),
    )
    return jax.shard_map(
        body, mesh=mesh, in_specs=placed, out_specs=P("member", None, "band", None), check_vma=False
    )
```

```python
import functools
import math

import jax
import jax.numpy as jnp
import numpy as np
from jax import lax
from jax.experimental import pallas as pl
from jax.experimental.pallas import tpu as pltpu
from jax.sharding import PartitionSpec as P

STEPS = 2
SHIFT = 44.0
GROUP = 8
ROWS = 16
VMEM = 56 * 1024 * 1024


def passed_along(value, axis, by):
    peers = lax.axis_size(axis)
    return lax.ppermute(value, axis, [(i, (i + by) % peers) for i in range(peers)])


def prepare(lon_ref, lat_ref, keep, south, lanes):
    first = lanes == 0
    for r in range(0, keep.shape[0], 8):
        cl = lon_ref[r : r + 8, :]
        ct = lat_ref[r : r + 8, :]
        keep[r : r + 8, :] = 1.0 - cl - ct
        south[r : r + 8, :] = jnp.where(first, 0.0, ct)


def two_steps(read, halo, edge_ref, lon_ref, keep, south, rows, lanes, emit):
    lat = keep.shape[1]
    top = rows == 0
    far = jnp.broadcast_to(halo[0:1, :], (8, lat))
    near = jnp.broadcast_to(halo[1:2, :], (8, lat))
    edge_lon = jnp.broadcast_to(edge_ref[0:1, :], (8, lat))
    edge_lat = jnp.broadcast_to(edge_ref[1:2, :], (8, lat))
    edge_keep = 1.0 - edge_lon - edge_lat
    edge_south = jnp.where(lanes == 0, 0.0, edge_lat)
    west0 = near
    west1 = edge_keep * near + edge_lon * far + edge_south * pltpu.roll(near, 1, 1)
    for r in range(0, keep.shape[0], 8):
        cells = read(r)
        ck = keep[r : r + 8, :]
        cs = south[r : r + 8, :]
        cl = lon_ref[r : r + 8, :]
        turned = pltpu.roll(cells, 1, 0)
        once = ck * cells + cl * jnp.where(top, west0, turned) + cs * pltpu.roll(cells, 1, 1)
        west0 = turned
        turned = pltpu.roll(once, 1, 0)
        twice = ck * once + cl * jnp.where(top, west1, turned) + cs * pltpu.roll(once, 1, 1)
        west1 = turned
        emit(r, twice)


def iotas(lat):
    return (
        lax.broadcasted_iota(jnp.int32, (8, lat), 0),
        lax.broadcasted_iota(jnp.int32, (8, lat), 1),
    )


def first_kernel(s_ref, h_ref, e_ref, lon_ref, lat_ref, f_ref, a_ref, t_ref, keep, south, diff):
    rows, lanes = iotas(keep.shape[1])

    @pl.when(pl.program_id(0) == 0)
    def _():
        prepare(lon_ref, lat_ref, keep, south, lanes)

    def emit(r, chunk):
        a_ref[0, r : r + 8, :] = chunk
        diff[r : r + 8, :] = f_ref[0, r : r + 8, :] - chunk

    two_steps(
        lambda r: s_ref[0, 0, r : r + 8, :], h_ref[0], e_ref, lon_ref, keep, south, rows, lanes, emit
    )
    t_ref[:, 0] = diff[...].T.reshape(t_ref.shape[0], t_ref.shape[2], t_ref.shape[3])


def rest_kernel(s_ref, h_ref, e_ref, lon_ref, lat_ref, o_ref, keep, south):
    rows, lanes = iotas(keep.shape[1])

    @pl.when((pl.program_id(0) == 0) & (pl.program_id(1) == 0))
    def _():
        prepare(lon_ref, lat_ref, keep, south, lanes)

    def one_level(i, carry):
        def emit(r, chunk):
            o_ref[0, i, r : r + 8, :] = chunk

        two_steps(
            lambda r: s_ref[0, i, r : r + 8, :],
            h_ref[0, i],
            e_ref,
            lon_ref,
            keep,
            south,
            rows,
            lanes,
            emit,
        )
        return carry

    lax.fori_loop(0, s_ref.shape[1], one_level, 0)


def last_kernel(a_ref, t_ref, b_ref, o_ref):
    lon, lat = a_ref.shape[1], a_ref.shape[2]
    o_ref[0, 0] = a_ref[0] + t_ref[:, 0].reshape(lat, lon).T


def table_kernel(start_ref, wave_ref, mu_ref, out_ref):
    half = mu_ref.shape[1]
    tiles = half // 128
    start = start_ref[...]
    mu = jnp.broadcast_to(mu_ref[...], (GROUP, half))
    wave = wave_ref[...]
    count = jnp.maximum(jnp.floor(start * (-1.0 / SHIFT)), 0.0)
    latest = jnp.exp(start + count * SHIFT)
    earlier = jnp.zeros_like(latest)
    before = jnp.ones_like(wave)

    def block(i, carry):
        latest, earlier, count, before = carry
        scale = jnp.exp(count * -SHIFT)
        for k in range(16):
            at = pl.multiple_of((i * 8 + k // 2) * GROUP, GROUP)
            row = latest * scale
            for c in range(tiles):
                out_ref[k % 2, c, pl.ds(at, GROUP), :] = row[:, c * 128 : (c + 1) * 128]
            offset = (i * 16 + (k + 1)).astype(jnp.float32)
            degree = wave + offset
            square = (4.0 * degree * degree - 1.0) / (offset * (degree + wave))
            factor = jnp.sqrt(square)
            older = factor / before
            before = factor
            wide = jnp.concatenate([factor] * tiles, axis=1)
            wide_old = jnp.concatenate([older] * tiles, axis=1)
            latest, earlier = wide * (mu * latest) - wide_old * earlier, latest
        grown = (jnp.maximum(jnp.abs(latest), jnp.abs(earlier)) > 1.0) & (count > 0.5)
        down = jnp.where(grown, math.exp(-SHIFT), 1.0)
        return latest * down, earlier * down, jnp.where(grown, count - 1.0, count), before

    lax.fori_loop(0, out_ref.shape[2] // (8 * GROUP), block, (latest, earlier, count, before))


def parts(x):
    high = x.astype(jnp.bfloat16)
    return high, (x - high.astype(jnp.float32)).astype(jnp.bfloat16)


def dot(a, b, dims):
    return lax.dot_general(a, b, (dims, ((), ())), preferred_element_type=jnp.float32)


def mirrored(x, flip):
    high, low = parts(x)
    both = ((1,), (0,))
    return dot(high, flip, both) + dot(low, flip, both)


def transform_kernel(firsts, stride, levels, *refs):
    f_ref, *p_refs = refs[: 1 + len(firsts)]
    r_ref, q_ref, j_ref, o_ref, even, odd = refs[1 + len(firsts) :]
    bands, width = f_ref.shape[0], f_ref.shape[2] // levels
    half = q_ref.shape[1]
    tiles = half // 128
    used = 2 * levels * GROUP
    pair_rows = 2 * GROUP
    flip = j_ref[...]
    quad = q_ref[...]
    across, along = ((1,), (1,)), ((1,), (0,))
    for number, (first, p_ref) in enumerate(zip(firsts, p_refs)):
        here = slice(number * pair_rows, (number + 1) * pair_rows)
        whole = jnp.concatenate(
            [
                jnp.concatenate(
                    [f_ref[s, here, v * width : (v + 1) * width] for s in range(bands)], axis=1
                )
                for v in range(levels)
            ],
            axis=0,
        )
        north = whole[:, :half]
        turned = mirrored(whole[:, half:], flip)
        plus = (north + turned) * quad
        minus = (north - turned) * quad
        for c in range(tiles):
            even[c, :used, :] = plus[:, c * 128 : (c + 1) * 128]
            odd[c, :used, :] = minus[:, c * 128 : (c + 1) * 128]
            if used < GROUP * ROWS:
                even[c, used:, :] = jnp.zeros((GROUP * ROWS - used, 128), jnp.float32)
                odd[c, used:, :] = jnp.zeros((GROUP * ROWS - used, 128), jnp.float32)
        length = p_ref.shape[2] // GROUP
        for m in range(GROUP):
            sums = []
            for p, side in ((0, even), (1, odd)):
                rows = [side[c, pl.ds(m, ROWS, stride=GROUP), :] for c in range(tiles)]
                f_high, f_low = parts(jnp.concatenate(rows, axis=1))
                table = [p_ref[p, c, pl.ds(m, length, stride=GROUP), :] for c in range(tiles)]
                p_high, p_low = parts(jnp.concatenate(table, axis=1))
                pair = dot(jnp.concatenate([f_high, f_low], axis=0), p_high, across)
                coeffs = pair[:ROWS] + pair[ROWS:] + dot(f_high, p_low, across)
                at = (first + m) * stride
                c_high, c_low = parts(coeffs * r_ref[p : p + 1, at : at + length])
                pair = dot(jnp.concatenate([c_high, c_low], axis=0), p_high, along)
                sums.append(pair[:ROWS] + pair[ROWS:] + dot(c_high, p_low, along))
            plus = sums[0] + sums[1]
            minus = sums[0] - sums[1]
            for c in range(tiles):
                even[c, pl.ds(m, ROWS, stride=GROUP), :] = plus[:, c * 128 : (c + 1) * 128]
                odd[c, pl.ds(m, ROWS, stride=GROUP), :] = minus[:, c * 128 : (c + 1) * 128]
        north = jnp.concatenate([even[c, :used, :] for c in range(tiles)], axis=1)
        south = jnp.concatenate([odd[c, :used, :] for c in range(tiles)], axis=1)
        whole = jnp.concatenate([north, mirrored(south, flip)], axis=1)
        for s in range(bands):
            o_ref[s, here, :] = jnp.concatenate(
                [
                    whole[v * pair_rows : (v + 1) * pair_rows, s * width : (s + 1) * width]
                    for v in range(levels)
                ],
                axis=1,
            )


def cost(flops, moved):
    return pl.CostEstimate(flops=int(flops), bytes_accessed=int(moved), transcendentals=0)


def body(state, courant_lon, courant_lat, reference_field, nudge_rate):
    fields, levels, lon, lat = state.shape
    bands = lax.axis_size("band")
    place = lax.axis_index("band")
    lon_total = lon * bands
    lat_local = lat // bands
    waves = nudge_rate.shape[0]
    wave_local = waves // bands
    groups = wave_local // GROUP
    half = lat // 2
    params = functools.partial(pltpu.CompilerParams, vmem_limit_bytes=VMEM)
    f32 = jnp.float32

    edges = passed_along(jnp.concatenate([courant_lon[-1:], courant_lat[-1:]], axis=0), "band", 1)
    halo0 = passed_along(state[0, :, -2:], "band", 1)
    halo1 = passed_along(state[1:, :, -2:], "band", 1)
    edges, halo0, halo1 = lax.optimization_barrier((edges, halo0, halo1))

    whole2 = lambda *_: (0, 0)
    courant_specs = [
        pl.BlockSpec((2, lat), whole2),
        pl.BlockSpec((lon, lat), whole2),
        pl.BlockSpec((lon, lat), whole2),
    ]
    coef_scratch = [pltpu.VMEM((lon, lat), f32), pltpu.VMEM((lon, lat), f32)]
    cells = levels * lon * lat
    advected0, turned = pl.pallas_call(
        first_kernel,
        grid=(levels,),
        in_specs=[
            pl.BlockSpec((1, 1, lon, lat), lambda v: (0, v, 0, 0)),
            pl.BlockSpec((1, 2, lat), lambda v: (v, 0, 0)),
            *courant_specs,
            pl.BlockSpec((1, lon, lat), lambda v: (v, 0, 0)),
        ],
        out_specs=[
            pl.BlockSpec((1, lon, lat), lambda v: (v, 0, 0)),
            pl.BlockSpec((bands, 1, lat_local, lon), lambda v: (0, v, 0, 0)),
        ],
        out_shape=[
            jax.ShapeDtypeStruct((levels, lon, lat), f32),
            jax.ShapeDtypeStruct((bands, levels, lat_local, lon), f32),
        ],
        scratch_shapes=[*coef_scratch, pltpu.VMEM((lon, lat), f32)],
        compiler_params=params(),
        cost_estimate=cost(cells * 14, cells * 16),
        name="advect_first",
    )(state, halo0, edges, courant_lon, courant_lat, reference_field)

    spread = lax.all_to_all(turned, "band", 0, 0, tiled=True)

    per = 3 if levels % 3 == 0 else 1
    partial = pl.pallas_call(
        rest_kernel,
        grid=(fields - 1, levels // per),
        in_specs=[
            pl.BlockSpec((1, per, lon, lat), lambda f, v: (f + 1, v, 0, 0)),
            pl.BlockSpec((1, per, 2, lat), lambda f, v: (f, v, 0, 0)),
            *courant_specs,
        ],
        out_specs=pl.BlockSpec((1, per, lon, lat), lambda f, v: (f + 1, v, 0, 0)),
        out_shape=jax.ShapeDtypeStruct(state.shape, f32),
        scratch_shapes=coef_scratch,
        compiler_params=params(),
        cost_estimate=cost((fields - 1) * cells * 14, (fields - 1) * cells * 8),
        name="advect_rest",
    )(state, halo1, edges, courant_lon, courant_lat)

    chunks = [
        sorted({g, groups - 1 - g}) for g in range((groups + 1) // 2)
    ]
    forward, inverse = [], []
    for chunk in chunks:
        steps = np.asarray(chunk)[:, None, None] * GROUP + np.arange(GROUP)[None, None, :]
        steps = np.broadcast_to(steps, (len(chunk), 2, GROUP)).reshape(-1)
        part = np.broadcast_to(np.arange(2)[None, :, None], (len(chunk), 2, GROUP)).reshape(-1)
        order = (np.arange(bands)[:, None] + bands * steps[None, :]).reshape(-1)
        part = np.tile(part, bands)[:, None]
        angle = (order[:, None] * np.arange(lon_total)[None, :] % lon_total) * (2 * np.pi / lon_total)
        values = np.where(part == 0, np.cos(angle), -np.sin(angle))
        doubling = np.where(order == 0, 1.0, 2.0)[:, None]
        forward.append(jnp.asarray((values / lon_total).astype(np.float32)))
        inverse.append(jnp.asarray((values * doubling).astype(np.float32)))
    theta = np.pi * (np.arange(half) + 0.5) / lat
    mu = jnp.asarray(np.cos(theta)[None].astype(np.float32))
    quad = jnp.asarray((np.sin(theta) * np.pi / lat)[None].astype(np.float32))
    log_sin = jnp.asarray(np.log(np.sin(theta)).astype(np.float32))
    k = np.arange(1, waves)
    norms = np.concatenate([[0.0], np.cumsum(np.log((2.0 * k + 1.0) / (2.0 * k)))])
    norms = norms.reshape(wave_local, bands).T.astype(np.float32)
    own_norm = lax.dynamic_slice_in_dim(jnp.asarray(norms), place, 1, 0)[0]
    own_wave = (place + bands * jnp.arange(wave_local)).astype(f32)
    starts = 0.5 * own_norm[:, None] + own_wave[:, None] * log_sin[None] - 0.5 * math.log(2.0)
    wide_wave = jnp.broadcast_to(own_wave[:, None], (wave_local, 128))
    flip = jnp.asarray(np.eye(half)[::-1].astype(np.float32)).astype(jnp.bfloat16)
    own_rate = lax.dynamic_slice_in_dim(
        jnp.concatenate([nudge_rate, jnp.zeros((waves + bands,), f32)]), place, 2 * waves, 0
    )

    own_rate = own_rate.reshape(waves, 2).T

    tables = []
    for g in range(groups):
        depth = waves - bands * GROUP * g
        depth = -(-depth // 16) * 16
        at = slice(g * GROUP, (g + 1) * GROUP)
        tables.append(
            pl.pallas_call(
                table_kernel,
                out_shape=jax.ShapeDtypeStruct((2, half // 128, depth // 2 * GROUP, 128), f32),
                compiler_params=params(),
                cost_estimate=cost(depth * GROUP * half * 8, depth * GROUP * half * 4),
                name="legendre_table",
            )(starts[at], wide_wave[at], mu)
        )

    spread, *tables = lax.optimization_barrier((spread, *tables))
    rows = [2 * GROUP * len(chunk) for chunk in chunks]
    increment = 0.0
    for n, chunk in enumerate(chunks):
        fourier = lax.dot_general(
            forward[n].reshape(bands * rows[n], bands, lon),
            spread,
            (((1, 2), (0, 3)), ((), ())),
            precision=lax.Precision.HIGH,
        )
        fourier = fourier.reshape(bands, rows[n], levels * lat_local)
        owned = lax.all_to_all(fourier, "band", 0, 0, tiled=True)
        depth = sum(tables[g].shape[2] for g in chunk)
        synth = pl.pallas_call(
            functools.partial(
                transform_kernel, tuple(g * GROUP for g in chunk), bands // 2, levels
            ),
            out_shape=jax.ShapeDtypeStruct(owned.shape, f32),
            scratch_shapes=[pltpu.VMEM((half // 128, GROUP * ROWS, 128), f32)] * 2,
            compiler_params=params(),
            cost_estimate=cost(depth * half * 600, depth * half * 8),
            name="legendre_transform",
        )(owned, *[tables[g] for g in chunk], own_rate, quad, flip)
        gathered = lax.all_to_all(synth, "band", 0, 0, tiled=True)
        increment = increment + lax.dot_general(
            gathered.reshape(bands * rows[n], levels * lat_local),
            inverse[n],
            (((0,), (0,)), ((), ())),
            precision=lax.Precision.HIGH,
        )
    increment = increment.reshape(levels * lat_local, bands, lon).transpose(1, 0, 2)
    increment = increment.reshape(bands, levels, lat_local, lon)
    increment = lax.all_to_all(increment, "band", 0, 0, tiled=True)

    return pl.pallas_call(
        last_kernel,
        grid=(levels,),
        in_specs=[
            pl.BlockSpec((1, lon, lat), lambda v: (v, 0, 0)),
            pl.BlockSpec((bands, 1, lat_local, lon), lambda v: (0, v, 0, 0)),
            pl.BlockSpec(memory_space=pl.ANY),
        ],
        out_specs=pl.BlockSpec((1, 1, lon, lat), lambda v: (0, v, 0, 0)),
        out_shape=jax.ShapeDtypeStruct(state.shape, f32),
        input_output_aliases={2: 0},
        compiler_params=params(),
        cost_estimate=cost(cells, cells * 12),
        name="add_increment",
    )(advected0, increment, partial)


def solution(mesh):
    placed = (
        P("member", None, "band", None),
        P(("member", "band"), None),
        P(("member", "band"), None),
        P("member", "band", None),
        P(),
    )
    return jax.shard_map(
        body, mesh=mesh, in_specs=placed, out_specs=P("member", None, "band", None), check_vma=False
    )
```

```python
import functools
import math

import jax
import jax.numpy as jnp
import numpy as np
from jax import lax
from jax.experimental import pallas as pl
from jax.experimental.pallas import tpu as pltpu
from jax.sharding import PartitionSpec as P

STEPS = 2
SHIFT = 44.0
GROUP = 8
ROWS = 16
VMEM = 56 * 1024 * 1024


def passed_along(value, axis, by):
    peers = lax.axis_size(axis)
    return lax.ppermute(value, axis, [(i, (i + by) % peers) for i in range(peers)])


def prepare(lon_ref, lat_ref, keep, south, lanes):
    first = lanes == 0
    for r in range(0, keep.shape[0], 8):
        cl = lon_ref[r : r + 8, :]
        ct = lat_ref[r : r + 8, :]
        keep[r : r + 8, :] = 1.0 - cl - ct
        south[r : r + 8, :] = jnp.where(first, 0.0, ct)


def two_steps(read, halo, edge_ref, lon_ref, keep, south, rows, lanes, emit):
    lat = keep.shape[1]
    top = rows == 0
    far = jnp.broadcast_to(halo[0:1, :], (8, lat))
    near = jnp.broadcast_to(halo[1:2, :], (8, lat))
    edge_lon = jnp.broadcast_to(edge_ref[0:1, :], (8, lat))
    edge_lat = jnp.broadcast_to(edge_ref[1:2, :], (8, lat))
    edge_keep = 1.0 - edge_lon - edge_lat
    edge_south = jnp.where(lanes == 0, 0.0, edge_lat)
    west0 = near
    west1 = edge_keep * near + edge_lon * far + edge_south * pltpu.roll(near, 1, 1)
    for r in range(0, keep.shape[0], 8):
        cells = read(r)
        ck = keep[r : r + 8, :]
        cs = south[r : r + 8, :]
        cl = lon_ref[r : r + 8, :]
        turned = pltpu.roll(cells, 1, 0)
        once = ck * cells + cl * jnp.where(top, west0, turned) + cs * pltpu.roll(cells, 1, 1)
        west0 = turned
        turned = pltpu.roll(once, 1, 0)
        twice = ck * once + cl * jnp.where(top, west1, turned) + cs * pltpu.roll(once, 1, 1)
        west1 = turned
        emit(r, twice)


def iotas(lat):
    return (
        lax.broadcasted_iota(jnp.int32, (8, lat), 0),
        lax.broadcasted_iota(jnp.int32, (8, lat), 1),
    )


def first_kernel(s_ref, h_ref, e_ref, lon_ref, lat_ref, f_ref, a_ref, t_ref, keep, south, diff):
    rows, lanes = iotas(keep.shape[1])

    @pl.when(pl.program_id(0) == 0)
    def _():
        prepare(lon_ref, lat_ref, keep, south, lanes)

    def emit(r, chunk):
        a_ref[0, r : r + 8, :] = chunk
        diff[r : r + 8, :] = f_ref[0, r : r + 8, :] - chunk

    two_steps(
        lambda r: s_ref[0, 0, r : r + 8, :], h_ref[0], e_ref, lon_ref, keep, south, rows, lanes, emit
    )
    t_ref[:, 0] = diff[...].T.reshape(t_ref.shape[0], t_ref.shape[2], t_ref.shape[3])


def rest_kernel(s_ref, h_ref, e_ref, lon_ref, lat_ref, o_ref, keep, south):
    rows, lanes = iotas(keep.shape[1])

    @pl.when((pl.program_id(0) == 0) & (pl.program_id(1) == 0))
    def _():
        prepare(lon_ref, lat_ref, keep, south, lanes)

    def one_level(i, carry):
        def emit(r, chunk):
            o_ref[0, i, r : r + 8, :] = chunk

        two_steps(
            lambda r: s_ref[0, i, r : r + 8, :],
            h_ref[0, i],
            e_ref,
            lon_ref,
            keep,
            south,
            rows,
            lanes,
            emit,
        )
        return carry

    lax.fori_loop(0, s_ref.shape[1], one_level, 0)


def last_kernel(a_ref, t_ref, b_ref, o_ref):
    lon, lat = a_ref.shape[1], a_ref.shape[2]
    o_ref[0, 0] = a_ref[0] + t_ref[:, 0].reshape(lat, lon).T


def table_kernel(start_ref, wave_ref, mu_ref, out_ref):
    half = mu_ref.shape[1]
    tiles = half // 128
    start = start_ref[...]
    mu = jnp.broadcast_to(mu_ref[...], (GROUP, half))
    wave = wave_ref[...]
    count = jnp.maximum(jnp.floor(start * (-1.0 / SHIFT)), 0.0)
    latest = jnp.exp(start + count * SHIFT)
    earlier = jnp.zeros_like(latest)
    before = jnp.ones_like(wave)

    def block(i, carry):
        latest, earlier, count, before = carry
        scale = jnp.exp(count * -SHIFT)
        for k in range(16):
            at = pl.multiple_of((i * 8 + k // 2) * GROUP, GROUP)
            row = latest * scale
            for c in range(tiles):
                out_ref[k % 2, c, pl.ds(at, GROUP), :] = row[:, c * 128 : (c + 1) * 128]
            offset = (i * 16 + (k + 1)).astype(jnp.float32)
            degree = wave + offset
            square = (4.0 * degree * degree - 1.0) / (offset * (degree + wave))
            factor = jnp.sqrt(square)
            older = factor / before
            before = factor
            wide = jnp.concatenate([factor] * tiles, axis=1)
            wide_old = jnp.concatenate([older] * tiles, axis=1)
            latest, earlier = wide * (mu * latest) - wide_old * earlier, latest
        grown = (jnp.maximum(jnp.abs(latest), jnp.abs(earlier)) > 1.0) & (count > 0.5)
        down = jnp.where(grown, math.exp(-SHIFT), 1.0)
        return latest * down, earlier * down, jnp.where(grown, count - 1.0, count), before

    lax.fori_loop(0, out_ref.shape[2] // (8 * GROUP), block, (latest, earlier, count, before))


def parts(x):
    high = x.astype(jnp.bfloat16)
    return high, (x - high.astype(jnp.float32)).astype(jnp.bfloat16)


def dot(a, b, dims):
    return lax.dot_general(a, b, (dims, ((), ())), preferred_element_type=jnp.float32)


def mirrored(x, flip):
    high, low = parts(x)
    both = ((1,), (0,))
    return dot(high, flip, both) + dot(low, flip, both)


def transform_kernel(firsts, stride, levels, *refs):
    f_ref, *p_refs = refs[: 1 + len(firsts)]
    r_ref, q_ref, j_ref, o_ref, even, odd = refs[1 + len(firsts) :]
    bands, width = f_ref.shape[0], f_ref.shape[2] // levels
    half = q_ref.shape[1]
    tiles = half // 128
    used = 2 * levels * GROUP
    pair_rows = 2 * GROUP
    flip = j_ref[...]
    quad = q_ref[...]
    across, along = ((1,), (1,)), ((1,), (0,))
    for number, (first, p_ref) in enumerate(zip(firsts, p_refs)):
        here = slice(number * pair_rows, (number + 1) * pair_rows)
        whole = jnp.concatenate(
            [
                jnp.concatenate(
                    [f_ref[s, here, v * width : (v + 1) * width] for s in range(bands)], axis=1
                )
                for v in range(levels)
            ],
            axis=0,
        )
        north = whole[:, :half]
        turned = mirrored(whole[:, half:], flip)
        plus = (north + turned) * quad
        minus = (north - turned) * quad
        for c in range(tiles):
            even[c, :used, :] = plus[:, c * 128 : (c + 1) * 128]
            odd[c, :used, :] = minus[:, c * 128 : (c + 1) * 128]
            if used < GROUP * ROWS:
                even[c, used:, :] = jnp.zeros((GROUP * ROWS - used, 128), jnp.float32)
                odd[c, used:, :] = jnp.zeros((GROUP * ROWS - used, 128), jnp.float32)
        length = p_ref.shape[2] // GROUP
        for m in range(GROUP):
            sums = []
            for p, side in ((0, even), (1, odd)):
                rows = [side[c, pl.ds(m, ROWS, stride=GROUP), :] for c in range(tiles)]
                f_high, f_low = parts(jnp.concatenate(rows, axis=1))
                table = [p_ref[p, c, pl.ds(m, length, stride=GROUP), :] for c in range(tiles)]
                p_high, p_low = parts(jnp.concatenate(table, axis=1))
                pair = dot(jnp.concatenate([f_high, f_low], axis=0), p_high, across)
                coeffs = pair[:ROWS] + pair[ROWS:] + dot(f_high, p_low, across)
                at = (first + m) * stride
                c_high, c_low = parts(coeffs * r_ref[p : p + 1, at : at + length])
                pair = dot(jnp.concatenate([c_high, c_low], axis=0), p_high, along)
                sums.append(pair[:ROWS] + pair[ROWS:] + dot(c_high, p_low, along))
            plus = sums[0] + sums[1]
            minus = sums[0] - sums[1]
            for c in range(tiles):
                even[c, pl.ds(m, ROWS, stride=GROUP), :] = plus[:, c * 128 : (c + 1) * 128]
                odd[c, pl.ds(m, ROWS, stride=GROUP), :] = minus[:, c * 128 : (c + 1) * 128]
        north = jnp.concatenate([even[c, :used, :] for c in range(tiles)], axis=1)
        south = jnp.concatenate([odd[c, :used, :] for c in range(tiles)], axis=1)
        whole = jnp.concatenate([north, mirrored(south, flip)], axis=1)
        for s in range(bands):
            o_ref[s, here, :] = jnp.concatenate(
                [
                    whole[v * pair_rows : (v + 1) * pair_rows, s * width : (s + 1) * width]
                    for v in range(levels)
                ],
                axis=1,
            )


def cost(flops, moved):
    return pl.CostEstimate(flops=int(flops), bytes_accessed=int(moved), transcendentals=0)


def body(state, courant_lon, courant_lat, reference_field, nudge_rate):
    fields, levels, lon, lat = state.shape
    bands = lax.axis_size("band")
    place = lax.axis_index("band")
    lon_total = lon * bands
    lat_local = lat // bands
    waves = nudge_rate.shape[0]
    wave_local = waves // bands
    groups = wave_local // GROUP
    half = lat // 2
    params = functools.partial(pltpu.CompilerParams, vmem_limit_bytes=VMEM)
    f32 = jnp.float32

    edges = passed_along(jnp.concatenate([courant_lon[-1:], courant_lat[-1:]], axis=0), "band", 1)
    halo0 = passed_along(state[0, :, -2:], "band", 1)
    halo1 = passed_along(state[1:, :, -2:], "band", 1)
    edges, halo0, halo1 = lax.optimization_barrier((edges, halo0, halo1))

    whole2 = lambda *_: (0, 0)
    courant_specs = [
        pl.BlockSpec((2, lat), whole2),
        pl.BlockSpec((lon, lat), whole2),
        pl.BlockSpec((lon, lat), whole2),
    ]
    coef_scratch = [pltpu.VMEM((lon, lat), f32), pltpu.VMEM((lon, lat), f32)]
    cells = levels * lon * lat
    advected0, turned = pl.pallas_call(
        first_kernel,
        grid=(levels,),
        in_specs=[
            pl.BlockSpec((1, 1, lon, lat), lambda v: (0, v, 0, 0)),
            pl.BlockSpec((1, 2, lat), lambda v: (v, 0, 0)),
            *courant_specs,
            pl.BlockSpec((1, lon, lat), lambda v: (v, 0, 0)),
        ],
        out_specs=[
            pl.BlockSpec((1, lon, lat), lambda v: (v, 0, 0)),
            pl.BlockSpec((bands, 1, lat_local, lon), lambda v: (0, v, 0, 0)),
        ],
        out_shape=[
            jax.ShapeDtypeStruct((levels, lon, lat), f32),
            jax.ShapeDtypeStruct((bands, levels, lat_local, lon), f32),
        ],
        scratch_shapes=[*coef_scratch, pltpu.VMEM((lon, lat), f32)],
        compiler_params=params(),
        cost_estimate=cost(cells * 14, cells * 16),
        name="advect_first",
    )(state, halo0, edges, courant_lon, courant_lat, reference_field)

    spread = lax.all_to_all(turned, "band", 0, 0, tiled=True)

    per = 3 if levels % 3 == 0 else 1
    partial = pl.pallas_call(
        rest_kernel,
        grid=(fields - 1, levels // per),
        in_specs=[
            pl.BlockSpec((1, per, lon, lat), lambda f, v: (f + 1, v, 0, 0)),
            pl.BlockSpec((1, per, 2, lat), lambda f, v: (f, v, 0, 0)),
            *courant_specs,
        ],
        out_specs=pl.BlockSpec((1, per, lon, lat), lambda f, v: (f + 1, v, 0, 0)),
        out_shape=jax.ShapeDtypeStruct(state.shape, f32),
        scratch_shapes=coef_scratch,
        compiler_params=params(),
        cost_estimate=cost((fields - 1) * cells * 14, (fields - 1) * cells * 8),
        name="advect_rest",
    )(state, halo1, edges, courant_lon, courant_lat)

    chunks = [
        sorted({g, groups - 1 - g}) for g in range((groups + 1) // 2)
    ]
    forward, inverse = [], []
    for chunk in chunks:
        steps = np.asarray(chunk)[:, None, None] * GROUP + np.arange(GROUP)[None, None, :]
        steps = np.broadcast_to(steps, (len(chunk), 2, GROUP)).reshape(-1)
        part = np.broadcast_to(np.arange(2)[None, :, None], (len(chunk), 2, GROUP)).reshape(-1)
        order = (np.arange(bands)[:, None] + bands * steps[None, :]).reshape(-1)
        part = np.tile(part, bands)[:, None]
        angle = (order[:, None] * np.arange(lon_total)[None, :] % lon_total) * (2 * np.pi / lon_total)
        values = np.where(part == 0, np.cos(angle), -np.sin(angle))
        doubling = np.where(order == 0, 1.0, 2.0)[:, None]
        forward.append(jnp.asarray((values / lon_total).astype(np.float32)))
        inverse.append(jnp.asarray((values * doubling).astype(np.float32)))
    theta = np.pi * (np.arange(half) + 0.5) / lat
    mu = jnp.asarray(np.cos(theta)[None].astype(np.float32))
    quad = jnp.asarray((np.sin(theta) * np.pi / lat)[None].astype(np.float32))
    log_sin = jnp.asarray(np.log(np.sin(theta)).astype(np.float32))
    k = np.arange(1, waves)
    norms = np.concatenate([[0.0], np.cumsum(np.log((2.0 * k + 1.0) / (2.0 * k)))])
    norms = norms.reshape(wave_local, bands).T.astype(np.float32)
    own_norm = lax.dynamic_slice_in_dim(jnp.asarray(norms), place, 1, 0)[0]
    own_wave = (place + bands * jnp.arange(wave_local)).astype(f32)
    starts = 0.5 * own_norm[:, None] + own_wave[:, None] * log_sin[None] - 0.5 * math.log(2.0)
    wide_wave = jnp.broadcast_to(own_wave[:, None], (wave_local, 128))
    flip = jnp.asarray(np.eye(half)[::-1].astype(np.float32)).astype(jnp.bfloat16)
    own_rate = lax.dynamic_slice_in_dim(
        jnp.concatenate([nudge_rate, jnp.zeros((waves + bands,), f32)]), place, 2 * waves, 0
    )

    own_rate = own_rate.reshape(waves, 2).T

    tables = []
    for g in range(groups):
        depth = waves - bands * GROUP * g
        depth = -(-depth // 16) * 16
        at = slice(g * GROUP, (g + 1) * GROUP)
        tables.append(
            pl.pallas_call(
                table_kernel,
                out_shape=jax.ShapeDtypeStruct((2, half // 128, depth // 2 * GROUP, 128), f32),
                compiler_params=params(),
                cost_estimate=cost(depth * GROUP * half * 8, depth * GROUP * half * 4),
                name="legendre_table",
            )(starts[at], wide_wave[at], mu)
        )

    spread, *tables = lax.optimization_barrier((spread, *tables))
    rows = [2 * GROUP * len(chunk) for chunk in chunks]
    circles = spread.reshape(bands, levels * lat_local, lon).transpose(1, 0, 2)
    circles = circles.reshape(levels * lat_local, lon_total)
    increment = 0.0
    for n, chunk in enumerate(chunks):
        fourier = lax.dot_general(
            forward[n],
            circles,
            (((1,), (1,)), ((), ())),
            precision=lax.Precision.HIGH,
        )
        fourier = fourier.reshape(bands, rows[n], levels * lat_local)
        owned = lax.all_to_all(fourier, "band", 0, 0, tiled=True)
        depth = sum(tables[g].shape[2] for g in chunk)
        synth = pl.pallas_call(
            functools.partial(
                transform_kernel, tuple(g * GROUP for g in chunk), bands // 2, levels
            ),
            out_shape=jax.ShapeDtypeStruct(owned.shape, f32),
            scratch_shapes=[pltpu.VMEM((half // 128, GROUP * ROWS, 128), f32)] * 2,
            compiler_params=params(),
            cost_estimate=cost(depth * half * 600, depth * half * 8),
            name="legendre_transform",
        )(owned, *[tables[g] for g in chunk], own_rate, quad, flip)
        gathered = lax.all_to_all(synth, "band", 0, 0, tiled=True)
        increment = increment + lax.dot_general(
            gathered.reshape(bands * rows[n], levels * lat_local),
            inverse[n],
            (((0,), (0,)), ((), ())),
            precision=lax.Precision.HIGH,
        )
    increment = increment.reshape(levels * lat_local, bands, lon).transpose(1, 0, 2)
    increment = increment.reshape(bands, levels, lat_local, lon)
    increment = lax.all_to_all(increment, "band", 0, 0, tiled=True)

    return pl.pallas_call(
        last_kernel,
        grid=(levels,),
        in_specs=[
            pl.BlockSpec((1, lon, lat), lambda v: (v, 0, 0)),
            pl.BlockSpec((bands, 1, lat_local, lon), lambda v: (0, v, 0, 0)),
            pl.BlockSpec(memory_space=pl.ANY),
        ],
        out_specs=pl.BlockSpec((1, 1, lon, lat), lambda v: (0, v, 0, 0)),
        out_shape=jax.ShapeDtypeStruct(state.shape, f32),
        input_output_aliases={2: 0},
        compiler_params=params(),
        cost_estimate=cost(cells, cells * 12),
        name="add_increment",
    )(advected0, increment, partial)


def solution(mesh):
    placed = (
        P("member", None, "band", None),
        P(("member", "band"), None),
        P(("member", "band"), None),
        P("member", "band", None),
        P(),
    )
    return jax.shard_map(
        body, mesh=mesh, in_specs=placed, out_specs=P("member", None, "band", None), check_vma=False
    )
```
